256 devices in a mesh: dp: 64 (over y, z, x_lo), tensor: 4 (over x_hi, core).
Axes of the slice: x: 4 (x_hi: 2, x_lo: 2; x = x_hi * 2 + x_lo), y: 4, z: 8, core: 2. Of those that a mesh axis runs over, the one named last changes fastest.
Arguments:
- pooled: bfloat16 [2, 8192, 1152], P(None, 'dp', 'tensor'), may hold values from -6 to 6
- ln_gain: bfloat16 [2, 1152], replicated, may hold values from 0.5 to 1.5
- ln_bias: bfloat16 [2, 1152], replicated, may hold values from -3 to 3
- fc1: bfloat16 [2, 1152, 4304], P(None, None, 'tensor'), may hold values from -0.1875 to 0.1875
- fc1_bias: bfloat16 [2, 4304], P(None, 'tensor'), may hold values from -3 to 3
- fc2: bfloat16 [2, 4304, 1152], P(None, 'tensor'), may hold values from -0.09375 to 0.09375
- fc2_bias: bfloat16 [2, 1152], replicated, may hold values from -1.1953125 to 1.1953125
- logit_scale: float32 [], replicated, may hold values from 8 to 12
- logit_bias: float32 [], replicated, may hold values from -3 to -1
- loss_scale: float32 [], replicated, may hold values from 8192 to 65536
Outputs:
- pooled_grad: bfloat16 [2, 8192, 1152], P(None, 'dp', 'tensor')
The draws below stay inside these ranges and needn't reach their ends.
All inputs are finite; a program needn't handle non-finite values.
Results may differ from the reference program's by a relative error of at most 0.0075.
Values may be sent and summed in bfloat16 or wider, within the bound.
No kernel may reach another device: no remote copies, remote signals or barrier semaphores. Data moves between devices by JAX's collectives and lax.ppermute only.
A program may use at most 128 MiB of HBM per device.

```python
import math
import jax
import jax.numpy as jnp
from jax import lax

D = 1152
FF = 4304
TOK_DEV = 128
TOKENS = 8192
N_DP = 64


def draw_pooled(key, part):
    key = jax.random.fold_in(key, 11)
    centre_key, first_key, second_key, pick_key, mix_key, strength_key = jax.random.split(key, 6)
    clusters = max(TOKENS // 8, 1)
    member_of = jax.random.randint(pick_key, (TOKENS,), 0, clusters).astype(jnp.int32)
    centres = jnp.clip(jax.random.normal(centre_key, (clusters, D), jnp.float32), -4.0, 4.0)
    own = jnp.clip(jax.random.normal(first_key, (TOKENS, D), jnp.float32), -4.0, 4.0)
    other = jnp.clip(jax.random.normal(second_key, (TOKENS, D), jnp.float32), -4.0, 4.0)
    strength = jax.random.uniform(strength_key, (TOKENS, 1), jnp.float32, 0.78, 0.92)
    mixing = jax.random.uniform(mix_key, (TOKENS, 1), jnp.float32, 0.2, 0.6)
    rest = jnp.sqrt(1.0 - strength * strength)
    shared = centres[member_of] * strength
    images = shared + rest * own
    texts = shared + rest * (mixing * own + jnp.sqrt(1.0 - mixing * mixing) * other)
    stacked = jnp.stack([images, texts])
    return jnp.clip(stacked, -6.0, 6.0).astype(jnp.bfloat16)


def levels(key, extent, cuts, low, high):
    factor_of, own = 1.0, jax.random.fold_in(key, 6)
    for axis_at, shards_of in cuts:
        draws = jnp.exp(jax.random.uniform(jax.random.fold_in(own, axis_at), (shards_of,), jnp.float32, low / len(cuts), high / len(cuts)))
        factor_of = factor_of * jnp.repeat(draws, extent[axis_at] // shards_of).reshape([-1 if axis == axis_at else 1 for axis in range(len(extent))])
    return factor_of


def noise(own_key, shape, deviation, most, shards=(), held_as=jnp.bfloat16):
    gain = levels(own_key, shape, shards, -0.22, 0.18) if shards else 1.0
    values = jax.random.normal(own_key, shape, jnp.float32) * deviation * gain
    return jnp.minimum(jnp.maximum(values, -most), most).astype(held_as)


def setup_inputs(seed: int = 0) -> dict:
    streams_of = jax.random.split(jax.random.key(seed), 11)
    return {
        "pooled": draw_pooled(jax.random.fold_in(streams_of[10], 71), 0),
        "ln_gain": jnp.clip(1.0 + 0.1 * jax.random.normal(streams_of[1], (2, D), jnp.float32), 0.5, 1.5).astype(jnp.bfloat16),
        "ln_bias": noise(streams_of[2], (2, D), 0.3, 3.0),
        "fc1": noise(streams_of[3], (2, D, FF), D ** -0.5, 0.1875, ((2, 4),)),
        "fc1_bias": noise(streams_of[4], (2, FF), 0.5, 3.0, ((1, 4),)),
        "fc2": noise(streams_of[5], (2, FF, D), FF ** -0.5, 0.09375, ((1, 4),)),
        "fc2_bias": noise(streams_of[6], (2, D), 0.2, 1.1953125),
        "logit_scale": jnp.clip(jax.random.uniform(streams_of[7], (), jnp.float32, 8.0, 12.0), 8.0, 12.0),
        "logit_bias": jnp.clip(jax.random.uniform(streams_of[8], (), jnp.float32, -3.0, -1.0), -3.0, -1.0),
        "loss_scale": jnp.clip(jnp.exp(jax.random.uniform(streams_of[9], (), jnp.float32, math.log(8192.0), math.log(65536.0))), 8192.0, 65536.0),
    }


def layer_stats(inputs):
    centred = inputs - lax.optimization_barrier(jnp.mean(inputs, axis=-1, keepdims=True))
    inverse = lax.rsqrt(lax.optimization_barrier(jnp.mean(centred * centred, axis=-1, keepdims=True)) + 1e-06)
    return (centred * inverse, inverse)

def gelu_tanh(values):
    return jax.nn.gelu(values, approximate=True)

def reference(pooled, ln_gain, ln_bias, fc1, fc1_bias, fc2, fc2_bias, logit_scale, logit_bias, loss_scale):
    inputs = pooled.astype(jnp.float32)
    standard, inverse = layer_stats(inputs)
    gains = ln_gain.astype(jnp.float32)[:, None, :]
    normed = (standard * gains + ln_bias.astype(jnp.float32)[:, None, :]).astype(jnp.bfloat16)
    preact = jnp.einsum('ktd,kdf->ktf', normed.astype(jnp.float32), fc1.astype(jnp.float32))
    preact = preact + fc1_bias.astype(jnp.float32)[:, None, :]
    hidden = gelu_tanh(preact).astype(jnp.bfloat16)
    blocks = inputs + jnp.einsum('ktf,kfe->kte', hidden.astype(jnp.float32), fc2.astype(jnp.float32))
    blocks = blocks + fc2_bias.astype(jnp.float32)[:, None, :]
    lengths = jnp.sqrt(lax.optimization_barrier(jnp.sum(blocks * blocks, axis=-1, keepdims=True)) + 1e-06)
    units = (blocks / lengths).astype(jnp.bfloat16)
    unit_float = units.astype(jnp.float32)
    factor = loss_scale * logit_scale / TOKENS
    texts = unit_float[1]
    text_ids = jnp.arange(TOKENS, dtype=jnp.int32)

    def visit(text_grad, item):
        images, index = item
        scores = jnp.einsum('id,jd->ij', images, texts)
        logits = logit_scale * scores + logit_bias
        image_ids = index * TOK_DEV + jnp.arange(TOK_DEV, dtype=jnp.int32)
        diagonal = (image_ids[:, None] == text_ids[None, :]).astype(jnp.float32)
        rounded = (factor * (jax.nn.sigmoid(logits) - diagonal)).astype(jnp.bfloat16)
        weights = lax.optimization_barrier(rounded).astype(jnp.float32)
        image_grad = jnp.einsum('ij,jd->id', weights, texts)
        return (text_grad + jnp.einsum('ij,id->jd', weights, images), image_grad)
    image_blocks = unit_float[0].reshape(N_DP, TOK_DEV, D)
    text_grad, image_grads = lax.scan(visit, jnp.zeros((TOKENS, D), jnp.float32), (image_blocks, jnp.arange(N_DP, dtype=jnp.int32)))
    unit_grad = jnp.stack([image_grads.reshape(TOKENS, D), text_grad])
    along = lax.optimization_barrier(jnp.sum(unit_float * unit_grad, axis=-1, keepdims=True))
    block_grad = (unit_grad - unit_float * along) / lengths
    block_low = block_grad.astype(jnp.bfloat16)
    hidden_grad = jnp.einsum('kte,kfe->ktf', block_low.astype(jnp.float32), fc2.astype(jnp.float32))
    _, gelu_back = jax.vjp(gelu_tanh, preact)
    preact_grad = gelu_back(hidden_grad)[0].astype(jnp.bfloat16)
    normed_grad = jnp.einsum('ktf,kdf->ktd', preact_grad.astype(jnp.float32), fc1.astype(jnp.float32))
    scaled = normed_grad * gains
    norm_grad = (scaled - lax.optimization_barrier(jnp.mean(scaled, axis=-1, keepdims=True)) - standard * lax.optimization_barrier(jnp.mean(scaled * standard, axis=-1, keepdims=True))) * inverse
    return (block_grad + norm_grad).astype(jnp.bfloat16)
```

```python
import functools

import jax
import jax.numpy as jnp
from jax import lax
from jax.experimental import pallas as pl
from jax.experimental.layout import Layout, with_layout_constraint
from jax.experimental.pallas import tpu as pltpu
from jax.sharding import Mesh
from jax.sharding import PartitionSpec as P

TENSOR = ("xh", "c")
DP = ("y", "z", "xl")
PLANE = ("y", "xl", "xh")
BF = jnp.bfloat16
F32 = jnp.float32


def layer_stats(inputs):
    centred = inputs - jnp.mean(inputs, axis=-1, keepdims=True)
    inverse = lax.rsqrt(jnp.mean(centred * centred, axis=-1, keepdims=True) + 1e-06)
    return (centred * inverse, inverse)


def gelu_tanh(values):
    return jax.nn.gelu(values, approximate=True)


def normalise(blocks):
    lengths = jnp.sqrt(jnp.sum(blocks * blocks, axis=-1, keepdims=True) + 1e-06)
    return (as_lies((blocks / lengths).astype(BF)), lengths)


def through_normalise(unit_grad, units, lengths):
    unit_grad = as_lies(unit_grad)
    units = units.astype(F32)
    along = jnp.sum(units * unit_grad, axis=-1, keepdims=True)
    return ((unit_grad - units * along) / lengths).astype(BF)


def as_lies(array):
    return with_layout_constraint(array, Layout(tuple(range(array.ndim))))


def hop(block, places):
    size = lax.axis_size("z")
    pairs = [
        ((z + (places, -places)[core]) % size * 2 + core, z * 2 + core)
        for z in range(size)
        for core in range(2)
    ]
    return as_lies(lax.ppermute(as_lies(block), ("z", "c"), pairs))


def exchange(parts, axes):
    return lax.all_to_all(parts, axes, 0, 0, tiled=True)


def swap(block, axis):
    return as_lies(lax.ppermute(as_lies(block), axis, [(0, 1), (1, 0)]))


def pick(array, index, axis):
    return lax.dynamic_index_in_dim(array, index, axis, keepdims=False)


def swap_sum(parts, name, axis):
    me = lax.axis_index(name)
    got = swap(pick(parts, 1 - me, axis).astype(BF), name)
    return pick(parts, me, axis).astype(F32) + got.astype(F32)


def in_order(own, other, name, axis):
    first = lax.axis_index(name) == 0
    return jnp.concatenate(
        [jnp.where(first, own, other), jnp.where(first, other, own)], axis=axis
    )


def swap_join(own, name, axis):
    return in_order(own, swap(own, name), name, axis)


def gather_ring(own, texts):
    half = own.shape[0]
    chip = swap_join(own, "c", 0)
    one, two = hop(chip, 1), hop(chip, 2)
    three = hop(two, 1)
    four = hop(lax.dynamic_slice_in_dim(two, lax.axis_index("c") * half, half, 0), 2)
    fetched = jnp.concatenate([one, two, three, four], axis=0)
    fetched, texts = lax.optimization_barrier((fetched, texts))
    return jnp.concatenate([chip, fetched, swap(fetched, "c")], axis=0), texts


def sum_ring(chip, fetched, other, texts):
    half = chip.shape[0] // 2
    fetched = fetched + swap(other, "c").astype(F32)
    one, two, three, four = jnp.split(fetched, [2 * half, 4 * half, 6 * half], axis=0)
    three = hop(three.astype(BF), -1).astype(F32)
    four = hop(four.astype(BF), -2).astype(F32)
    one = hop(one.astype(BF), -1).astype(F32)
    first = lax.axis_index("c") == 0
    none = jnp.zeros_like(four)
    two = two + three
    two = two + jnp.concatenate([jnp.where(first, four, none), jnp.where(first, none, four)])
    two = hop(two.astype(BF), -2).astype(F32)
    own, texts = lax.optimization_barrier((chip + one + two, texts))
    return swap_sum(own.reshape(2, half, -1), "c", 0), texts


def loss_kernel(
    part_rows, scalars, first, images, texts, chip, fetched, other, text_part, image_sum
):
    tile = 256
    for start in range(0, texts.shape[0], tile):
        block = texts[pl.ds(start, tile), :]
        scores = lax.dot_general(
            images[...], block, (((1,), (1,)), ((), ())), preferred_element_type=F32
        )
        logits = scalars[0] * scores + scalars[1]
        at_image = lax.broadcasted_iota(jnp.int32, scores.shape, 0) - first[0]
        at_text = lax.broadcasted_iota(jnp.int32, scores.shape, 1) + (start - first[1])
        diagonal = (at_image == at_text) & (at_image >= 0) & (at_image < part_rows)
        diagonal = diagonal.astype(F32)
        weights = (scalars[2] * (jax.nn.sigmoid(logits) - diagonal)).astype(BF)
        text_part[pl.ds(start, tile), :] = lax.dot_general(
            weights, images[...], (((0,), (0,)), ((), ())), preferred_element_type=F32
        ).astype(BF)
        product = jnp.dot(weights, block, preferred_element_type=F32)
        if start == 0:
            image_sum[...] = product
        else:
            image_sum[...] += product
    at_fetched, at_other = chip.shape[0], chip.shape[0] + fetched.shape[0]
    chip[...] = image_sum[:at_fetched, :]
    fetched[...] = image_sum[at_fetched:at_other, :]
    other[...] = image_sum[at_other:, :].astype(BF)


def loss_block(scalars, first, images, texts, part_rows):
    rows, dim = images.shape
    fetched = rows // 2 - part_rows
    whole = pl.BlockSpec(memory_space=pltpu.VMEM)
    small = pl.BlockSpec(memory_space=pltpu.SMEM)
    return pl.pallas_call(
        functools.partial(loss_kernel, part_rows),
        in_specs=[small, small, whole, whole],
        out_specs=[whole] * 4,
        out_shape=[
            jax.ShapeDtypeStruct((2 * part_rows, dim), F32),
            jax.ShapeDtypeStruct((fetched, dim), F32),
            jax.ShapeDtypeStruct((fetched, dim), BF),
            jax.ShapeDtypeStruct(texts.shape, BF),
        ],
        scratch_shapes=[pltpu.VMEM((rows, dim), F32)],
        compiler_params=pltpu.CompilerParams(vmem_limit_bytes=20 * 1024 * 1024),
        cost_estimate=pl.CostEstimate(
            flops=6 * rows * texts.shape[0] * dim,
            bytes_accessed=10 * rows * dim,
            transcendentals=rows * texts.shape[0],
        ),
    )(scalars, first, images, texts)


def on_device(
    pooled, ln_gain, ln_bias, fc1, fc1_bias, fc2, fc2_bias, logit_scale, logit_bias, loss_scale
):
    rows, width = pooled.shape[1], pooled.shape[2]
    member = lax.axis_index(TENSOR)
    part_rows = rows // lax.axis_size(TENSOR)
    tokens_all = rows * lax.axis_size(DP)

    own = jnp.swapaxes(pooled, 1, 2)
    far = swap(own, "xh")
    whole = in_order(own[:, None, None], far[:, None, None], "xh", 1)
    whole = swap_join(whole, "c", 2).reshape(2, 4 * width, rows)
    whole, ln_gain, ln_bias, fc1_bias, fc2_bias = lax.optimization_barrier(
        (whole, ln_gain, ln_bias, fc1_bias, fc2_bias)
    )
    inputs = jnp.swapaxes(whole, 1, 2).astype(F32)
    dim = inputs.shape[2]
    standard, inverse = layer_stats(inputs)
    gains = ln_gain.astype(F32)[:, None, :]
    normed = (standard * gains + ln_bias.astype(F32)[:, None, :]).astype(BF)
    preact = jnp.einsum("ktd,kdf->ktf", normed, fc1, preferred_element_type=F32)
    preact = preact + fc1_bias.astype(F32)[:, None, :]
    hidden = gelu_tanh(preact).astype(BF)
    partial = as_lies(jnp.einsum("ktf,kfe->kte", hidden, fc2, preferred_element_type=F32))

    quarter = lax.axis_index("c") * 2 + lax.axis_index("xh")
    partial = swap_sum(partial.reshape(2, 2, 2 * part_rows, dim), "c", 1)
    summed = swap_sum(partial.reshape(2, 2, part_rows, dim), "xh", 1)
    own_inputs = as_lies(lax.dynamic_slice_in_dim(inputs, quarter * part_rows, part_rows, 1))
    units, lengths = normalise(own_inputs + summed + fc2_bias.astype(F32)[:, None, :])

    n_text = lax.axis_size(PLANE)
    texts = exchange(jnp.broadcast_to(units[1], (n_text, part_rows, dim)), PLANE)
    texts = texts.reshape(n_text * part_rows, dim)
    images, texts = gather_ring(units[0], texts)
    factor = loss_scale * logit_scale / tokens_all
    scalars = jnp.stack([logit_scale, logit_bias, factor]).astype(F32)
    first = jnp.stack([lax.axis_index("c"), lax.axis_index(PLANE)]).astype(jnp.int32) * part_rows
    chip_part, fetched_part, other_part, text_part = loss_block(
        scalars, first, images, texts, part_rows
    )
    text_part = exchange(text_part.reshape(n_text, part_rows, dim), PLANE)
    image_grad, text_part = sum_ring(chip_part, fetched_part, other_part, text_part)
    text_grad = jnp.sum(text_part.astype(F32), axis=0)

    block_own = through_normalise(jnp.stack([image_grad, text_grad]), units, lengths)
    block_own = as_lies(block_own)
    block_low = as_lies(swap_join(as_lies(swap_join(block_own, "xh", 1)), "c", 1))
    hidden_grad = jnp.einsum("kte,kfe->ktf", block_low, fc2, preferred_element_type=F32)
    _, gelu_back = jax.vjp(gelu_tanh, preact)
    preact_grad = lax.optimization_barrier(gelu_back(hidden_grad)[0].astype(BF))
    normed_grad = jnp.einsum("ktf,kdf->ktd", preact_grad, fc1, preferred_element_type=F32)
    scaled = normed_grad * gains
    norm_term = (
        scaled
        - jnp.mean(scaled, axis=-1, keepdims=True)
        - standard * jnp.mean(scaled * standard, axis=-1, keepdims=True)
    ) * inverse
    norm_parts = as_lies(jnp.swapaxes(norm_term, 1, 2)).reshape(2, 2, 2, width, rows)
    norm_parts = as_lies(swap_sum(norm_parts, "c", 2))
    norm_share = as_lies(swap_sum(norm_parts, "xh", 1))
    block_share = as_lies(lax.dynamic_slice_in_dim(block_low, member * width, width, 2))
    block_share = as_lies(jnp.swapaxes(block_share, 1, 2)).astype(F32)
    return jnp.swapaxes(as_lies((block_share + norm_share).astype(BF)), 1, 2)


def solution(mesh):
    fine = Mesh(mesh.devices.reshape(4, 8, 2, 2, 2), ("y", "z", "xl", "xh", "c"))
    in_specs = (
        P(None, DP, TENSOR),
        P(),
        P(),
        P(None, None, TENSOR),
        P(None, TENSOR),
        P(None, TENSOR, None),
        P(),
        P(),
        P(),
        P(),
    )
    return jax.shard_map(
        on_device, mesh=fine, in_specs=in_specs, out_specs=P(None, DP, TENSOR), check_vma=False
    )
```

```python
import functools

import jax
import jax.numpy as jnp
from jax import lax
from jax.experimental import pallas as pl
from jax.experimental.layout import Layout, with_layout_constraint
from jax.experimental.pallas import tpu as pltpu
from jax.sharding import Mesh
from jax.sharding import PartitionSpec as P

TENSOR = ("xh", "c")
DP = ("y", "z", "xl")
PLANE = ("y", "xl", "xh")
BF = jnp.bfloat16
F32 = jnp.float32


def layer_stats(inputs):
    centred = inputs - jnp.mean(inputs, axis=-1, keepdims=True)
    inverse = lax.rsqrt(jnp.mean(centred * centred, axis=-1, keepdims=True) + 1e-06)
    return (centred * inverse, inverse)


def gelu_tanh(values):
    return jax.nn.gelu(values, approximate=True)


def normalise(blocks):
    lengths = jnp.sqrt(jnp.sum(blocks * blocks, axis=-1, keepdims=True) + 1e-06)
    return (as_lies((blocks / lengths).astype(BF)), lengths)


def through_normalise(unit_grad, units, lengths):
    unit_grad = as_lies(unit_grad)
    units = units.astype(F32)
    along = jnp.sum(units * unit_grad, axis=-1, keepdims=True)
    return ((unit_grad - units * along) / lengths).astype(BF)


def as_lies(array):
    return with_layout_constraint(array, Layout(tuple(range(array.ndim))))


def hop(block, places):
    size = lax.axis_size("z")
    pairs = [
        ((z + (places, -places)[core]) % size * 2 + core, z * 2 + core)
        for z in range(size)
        for core in range(2)
    ]
    return as_lies(lax.ppermute(as_lies(block), ("z", "c"), pairs))


def exchange(parts, axes):
    return lax.all_to_all(parts, axes, 0, 0, tiled=True)


def swap(block, axis):
    return as_lies(lax.ppermute(as_lies(block), axis, [(0, 1), (1, 0)]))


def pick(array, index, axis):
    return lax.dynamic_index_in_dim(array, index, axis, keepdims=False)


def swap_sum(parts, name, axis):
    me = lax.axis_index(name)
    got = swap(pick(parts, 1 - me, axis).astype(BF), name)
    return pick(parts, me, axis).astype(F32) + got.astype(F32)


def in_order(own, other, name, axis):
    first = lax.axis_index(name) == 0
    return jnp.concatenate(
        [jnp.where(first, own, other), jnp.where(first, other, own)], axis=axis
    )


def swap_join(own, name, axis):
    return in_order(own, swap(own, name), name, axis)


def gather_ring(own, texts):
    half = own.shape[0]
    chip = swap_join(own, "c", 0)
    one, two = hop(chip, 1), hop(chip, 2)
    three = hop(two, 1)
    four = hop(lax.dynamic_slice_in_dim(two, lax.axis_index("c") * half, half, 0), 2)
    fetched = jnp.concatenate([one, two, three, four], axis=0)
    fetched, texts = lax.optimization_barrier((fetched, texts))
    return jnp.concatenate([chip, fetched, swap(fetched, "c")], axis=0), texts


def sum_ring(chip, fetched, other, texts):
    half = chip.shape[0] // 2
    fetched = fetched + swap(other, "c").astype(F32)
    one, two, three, four = jnp.split(fetched, [2 * half, 4 * half, 6 * half], axis=0)
    three = hop(three.astype(BF), -1).astype(F32)
    four = hop(four.astype(BF), -2).astype(F32)
    one = hop(one.astype(BF), -1).astype(F32)
    first = lax.axis_index("c") == 0
    none = jnp.zeros_like(four)
    two = two + three
    two = two + jnp.concatenate([jnp.where(first, four, none), jnp.where(first, none, four)])
    two = hop(two.astype(BF), -2).astype(F32)
    own, texts = lax.optimization_barrier((chip + one + two, texts))
    return swap_sum(own.reshape(2, half, -1), "c", 0), texts


def loss_kernel(part_rows, scalars, first, images, texts, chip, fetched, other, text_part):
    scores = lax.dot_general(
        images[...], texts[...], (((1,), (1,)), ((), ())), preferred_element_type=F32
    )
    logits = scalars[0] * scores + scalars[1]
    at_image = lax.broadcasted_iota(jnp.int32, scores.shape, 0) - first[0]
    at_text = lax.broadcasted_iota(jnp.int32, scores.shape, 1) - first[1]
    diagonal = (at_image == at_text) & (at_image >= 0) & (at_image < part_rows)
    weights = (scalars[2] * (jax.nn.sigmoid(logits) - diagonal.astype(F32))).astype(BF)
    text_part[...] = lax.dot_general(
        weights, images[...], (((0,), (0,)), ((), ())), preferred_element_type=F32
    ).astype(BF)
    image_part = jnp.dot(weights, texts[...], preferred_element_type=F32)
    at_fetched, at_other = chip.shape[0], chip.shape[0] + fetched.shape[0]
    chip[...] = image_part[:at_fetched, :]
    fetched[...] = image_part[at_fetched:at_other, :]
    other[...] = image_part[at_other:, :].astype(BF)


def loss_block(scalars, first, images, texts, part_rows):
    rows, dim = images.shape
    fetched = rows // 2 - part_rows
    whole = pl.BlockSpec(memory_space=pltpu.VMEM)
    small = pl.BlockSpec(memory_space=pltpu.SMEM)
    return pl.pallas_call(
        functools.partial(loss_kernel, part_rows),
        in_specs=[small, small, whole, whole],
        out_specs=[whole] * 4,
        out_shape=[
            jax.ShapeDtypeStruct((2 * part_rows, dim), F32),
            jax.ShapeDtypeStruct((fetched, dim), F32),
            jax.ShapeDtypeStruct((fetched, dim), BF),
            jax.ShapeDtypeStruct(texts.shape, BF),
        ],
        compiler_params=pltpu.CompilerParams(vmem_limit_bytes=20 * 1024 * 1024),
        cost_estimate=pl.CostEstimate(
            flops=6 * rows * texts.shape[0] * dim,
            bytes_accessed=10 * rows * dim,
            transcendentals=rows * texts.shape[0],
        ),
    )(scalars, first, images, texts)


def on_device(
    pooled, ln_gain, ln_bias, fc1, fc1_bias, fc2, fc2_bias, logit_scale, logit_bias, loss_scale
):
    rows, width = pooled.shape[1], pooled.shape[2]
    member = lax.axis_index(TENSOR)
    part_rows = rows // lax.axis_size(TENSOR)
    tokens_all = rows * lax.axis_size(DP)

    own = jnp.swapaxes(pooled, 1, 2)
    far = swap(own, "xh")
    none = jnp.zeros_like(own)
    mine = in_order(own[:, None, None], none[:, None, None], "xh", 1)
    far, mine = lax.optimization_barrier((far, mine))
    whole = mine + in_order(none[:, None, None], far[:, None, None], "xh", 1)
    whole = swap_join(whole, "c", 2).reshape(2, 4 * width, rows)
    whole, ln_gain, ln_bias, fc1_bias, fc2_bias = lax.optimization_barrier(
        (whole, ln_gain, ln_bias, fc1_bias, fc2_bias)
    )
    inputs = jnp.swapaxes(whole, 1, 2).astype(F32)
    dim = inputs.shape[2]
    standard, inverse = layer_stats(inputs)
    gains = ln_gain.astype(F32)[:, None, :]
    normed = (standard * gains + ln_bias.astype(F32)[:, None, :]).astype(BF)
    preact = jnp.einsum("ktd,kdf->ktf", normed, fc1, preferred_element_type=F32)
    preact = preact + fc1_bias.astype(F32)[:, None, :]
    hidden = gelu_tanh(preact).astype(BF)
    partial = as_lies(jnp.einsum("ktf,kfe->kte", hidden, fc2, preferred_element_type=F32))

    quarter = lax.axis_index("c") * 2 + lax.axis_index("xh")
    partial = swap_sum(partial.reshape(2, 2, 2 * part_rows, dim), "c", 1)
    summed = swap_sum(partial.reshape(2, 2, part_rows, dim), "xh", 1)
    own_inputs = as_lies(lax.dynamic_slice_in_dim(inputs, quarter * part_rows, part_rows, 1))
    units, lengths = normalise(own_inputs + summed + fc2_bias.astype(F32)[:, None, :])

    n_text = lax.axis_size(PLANE)
    texts = exchange(jnp.broadcast_to(units[1], (n_text, part_rows, dim)), PLANE)
    texts = texts.reshape(n_text * part_rows, dim)
    images, texts = gather_ring(units[0], texts)
    factor = loss_scale * logit_scale / tokens_all
    scalars = jnp.stack([logit_scale, logit_bias, factor]).astype(F32)
    first = jnp.stack([lax.axis_index("c"), lax.axis_index(PLANE)]).astype(jnp.int32) * part_rows
    chip_part, fetched_part, other_part, text_part = loss_block(
        scalars, first, images, texts, part_rows
    )
    text_part = exchange(text_part.reshape(n_text, part_rows, dim), PLANE)
    image_grad, text_part = sum_ring(chip_part, fetched_part, other_part, text_part)
    text_grad = jnp.sum(text_part.astype(F32), axis=0)

    block_own = through_normalise(jnp.stack([image_grad, text_grad]), units, lengths)
    block_own = as_lies(block_own)
    block_low = as_lies(swap_join(as_lies(swap_join(block_own, "xh", 1)), "c", 1))
    hidden_grad = jnp.einsum("kte,kfe->ktf", block_low, fc2, preferred_element_type=F32)
    _, gelu_back = jax.vjp(gelu_tanh, preact)
    preact_grad = lax.optimization_barrier(gelu_back(hidden_grad)[0].astype(BF))
    normed_grad = jnp.einsum("ktf,kdf->ktd", preact_grad, fc1, preferred_element_type=F32)
    scaled = normed_grad * gains
    norm_term = (
        scaled
        - jnp.mean(scaled, axis=-1, keepdims=True)
        - standard * jnp.mean(scaled * standard, axis=-1, keepdims=True)
    ) * inverse
    norm_parts = as_lies(jnp.swapaxes(norm_term, 1, 2)).reshape(2, 2, 2, width, rows)
    norm_parts = as_lies(swap_sum(norm_parts, "c", 2))
    norm_share = as_lies(swap_sum(norm_parts, "xh", 1))
    block_share = as_lies(lax.dynamic_slice_in_dim(block_low, member * width, width, 2))
    block_share = as_lies(jnp.swapaxes(block_share, 1, 2)).astype(F32)
    return jnp.swapaxes(as_lies((block_share + norm_share).astype(BF)), 1, 2)


def solution(mesh):
    fine = Mesh(mesh.devices.reshape(4, 8, 2, 2, 2), ("y", "z", "xl", "xh", "c"))
    in_specs = (
        P(None, DP, TENSOR),
        P(),
        P(),
        P(None, None, TENSOR),
        P(None, TENSOR),
        P(None, TENSOR, None),
        P(),
        P(),
        P(),
        P(),
    )
    return jax.shard_map(
        on_device, mesh=fine, in_specs=in_specs, out_specs=P(None, DP, TENSOR), check_vma=False
    )
```

```python
import functools

import jax
import jax.numpy as jnp
from jax import lax
from jax.experimental import pallas as pl
from jax.experimental.layout import Layout, with_layout_constraint
from jax.experimental.pallas import tpu as pltpu
from jax.sharding import Mesh
from jax.sharding import PartitionSpec as P

TENSOR = ("xh", "c")
DP = ("y", "z", "xl")
PLANE = ("y", "xl", "xh")
BF = jnp.bfloat16
F32 = jnp.float32


def layer_stats(inputs):
    centred = inputs - jnp.mean(inputs, axis=-1, keepdims=True)
    inverse = lax.rsqrt(jnp.mean(centred * centred, axis=-1, keepdims=True) + 1e-06)
    return (centred * inverse, inverse)


def gelu_tanh(values):
    return jax.nn.gelu(values, approximate=True)


def normalise(blocks):
    lengths = jnp.sqrt(jnp.sum(blocks * blocks, axis=-1, keepdims=True) + 1e-06)
    return (as_lies((blocks / lengths).astype(BF)), lengths)


def through_normalise(unit_grad, units, lengths):
    unit_grad = as_lies(unit_grad)
    units = units.astype(F32)
    along = jnp.sum(units * unit_grad, axis=-1, keepdims=True)
    return ((unit_grad - units * along) / lengths).astype(BF)


def as_lies(array):
    return with_layout_constraint(array, Layout(tuple(range(array.ndim))))


def hop(block, places):
    size = lax.axis_size("z")
    pairs = [
        ((z + (places, -places)[core]) % size * 2 + core, z * 2 + core)
        for z in range(size)
        for core in range(2)
    ]
    return as_lies(lax.ppermute(as_lies(block), ("z", "c"), pairs))


def exchange(parts, axes):
    return lax.all_to_all(parts, axes, 0, 0, tiled=True)


def swap(block, axis):
    return as_lies(lax.ppermute(as_lies(block), axis, [(0, 1), (1, 0)]))


def pick(array, index, axis):
    return lax.dynamic_index_in_dim(array, index, axis, keepdims=False)


def swap_sum(parts, name, axis):
    me = lax.axis_index(name)
    got = swap(pick(parts, 1 - me, axis).astype(BF), name)
    return pick(parts, me, axis).astype(F32) + got.astype(F32)


def in_order(own, other, name, axis):
    first = lax.axis_index(name) == 0
    return jnp.concatenate(
        [jnp.where(first, own, other), jnp.where(first, other, own)], axis=axis
    )


def swap_join(own, name, axis):
    return in_order(own, swap(own, name), name, axis)


def gather_ring(own, texts):
    half = own.shape[0]
    chip = swap_join(own, "c", 0)
    one, two = hop(chip, 1), hop(chip, 2)
    three = hop(two, 1)
    four = hop(lax.dynamic_slice_in_dim(two, lax.axis_index("c") * half, half, 0), 2)
    fetched = jnp.concatenate([one, two, three, four], axis=0)
    fetched, texts = lax.optimization_barrier((fetched, texts))
    return jnp.concatenate([chip, fetched, swap(fetched, "c")], axis=0), texts


def sum_ring(chip, fetched, other, texts):
    half = chip.shape[0] // 2
    fetched = fetched.astype(F32) + swap(other, "c").astype(F32)
    one, two, three, four = jnp.split(fetched, [2 * half, 4 * half, 6 * half], axis=0)
    three = hop(three.astype(BF), -1).astype(F32)
    four = hop(four.astype(BF), -2)
    one, four = lax.optimization_barrier((one.astype(BF), four))
    one = hop(one, -1).astype(F32)
    four = four.astype(F32)
    first = lax.axis_index("c") == 0
    none = jnp.zeros_like(four)
    two = two + three
    two = two + jnp.concatenate([jnp.where(first, four, none), jnp.where(first, none, four)])
    two = hop(two.astype(BF), -2).astype(F32)
    own, texts = lax.optimization_barrier((chip + one + two, texts))
    return swap_sum(own.reshape(2, half, -1), "c", 0), texts


def loss_kernel(part_rows, scalars, first, images, texts, chip, fetched, other, text_part):
    scores = lax.dot_general(
        images[...], texts[...], (((1,), (1,)), ((), ())), preferred_element_type=F32
    )
    logits = scalars[0] * scores + scalars[1]
    at_image = lax.broadcasted_iota(jnp.int32, scores.shape, 0) - first[0]
    at_text = lax.broadcasted_iota(jnp.int32, scores.shape, 1) - first[1]
    diagonal = (at_image == at_text) & (at_image >= 0) & (at_image < part_rows)
    weights = (scalars[2] * (jax.nn.sigmoid(logits) - diagonal.astype(F32))).astype(BF)
    text_part[...] = lax.dot_general(
        weights, images[...], (((0,), (0,)), ((), ())), preferred_element_type=F32
    ).astype(BF)
    image_part = jnp.dot(weights, texts[...], preferred_element_type=F32)
    at_fetched, at_other = chip.shape[0], chip.shape[0] + fetched.shape[0]
    chip[...] = image_part[:at_fetched, :]
    fetched[...] = image_part[at_fetched:at_other, :].astype(BF)
    other[...] = image_part[at_other:, :].astype(BF)


def loss_block(scalars, first, images, texts, part_rows):
    rows, dim = images.shape
    fetched = rows // 2 - part_rows
    whole = pl.BlockSpec(memory_space=pltpu.VMEM)
    small = pl.BlockSpec(memory_space=pltpu.SMEM)
    return pl.pallas_call(
        functools.partial(loss_kernel, part_rows),
        in_specs=[small, small, whole, whole],
        out_specs=[whole] * 4,
        out_shape=[
            jax.ShapeDtypeStruct((2 * part_rows, dim), F32),
            jax.ShapeDtypeStruct((fetched, dim), BF),
            jax.ShapeDtypeStruct((fetched, dim), BF),
            jax.ShapeDtypeStruct(texts.shape, BF),
        ],
        compiler_params=pltpu.CompilerParams(vmem_limit_bytes=20 * 1024 * 1024),
        cost_estimate=pl.CostEstimate(
            flops=6 * rows * texts.shape[0] * dim,
            bytes_accessed=10 * rows * dim,
            transcendentals=rows * texts.shape[0],
        ),
    )(scalars, first, images, texts)


def on_device(
    pooled, ln_gain, ln_bias, fc1, fc1_bias, fc2, fc2_bias, logit_scale, logit_bias, loss_scale
):
    rows, width = pooled.shape[1], pooled.shape[2]
    member = lax.axis_index(TENSOR)
    part_rows = rows // lax.axis_size(TENSOR)
    tokens_all = rows * lax.axis_size(DP)

    own = jnp.swapaxes(pooled, 1, 2)
    far = swap(own, "xh")
    none = jnp.zeros_like(own)
    mine = in_order(own[:, None, None], none[:, None, None], "xh", 1)
    far, mine = lax.optimization_barrier((far, mine))
    whole = mine + in_order(none[:, None, None], far[:, None, None], "xh", 1)
    whole = swap_join(whole, "c", 2).reshape(2, 4 * width, rows)
    whole, ln_gain, ln_bias, fc1_bias, fc2_bias = lax.optimization_barrier(
        (whole, ln_gain, ln_bias, fc1_bias, fc2_bias)
    )
    inputs = jnp.swapaxes(whole, 1, 2).astype(F32)
    dim = inputs.shape[2]
    standard, inverse = layer_stats(inputs)
    gains = ln_gain.astype(F32)[:, None, :]
    normed = (standard * gains + ln_bias.astype(F32)[:, None, :]).astype(BF)
    preact = jnp.einsum("ktd,kdf->ktf", normed, fc1, preferred_element_type=F32)
    preact = preact + fc1_bias.astype(F32)[:, None, :]
    hidden = gelu_tanh(preact).astype(BF)
    partial = as_lies(jnp.einsum("ktf,kfe->kte", hidden, fc2, preferred_element_type=F32))

    quarter = lax.axis_index("c") * 2 + lax.axis_index("xh")
    partial = swap_sum(partial.reshape(2, 2, 2 * part_rows, dim), "c", 1)
    summed = swap_sum(partial.reshape(2, 2, part_rows, dim), "xh", 1)
    own_inputs = as_lies(lax.dynamic_slice_in_dim(inputs, quarter * part_rows, part_rows, 1))
    units, lengths = normalise(own_inputs + summed + fc2_bias.astype(F32)[:, None, :])

    n_text = lax.axis_size(PLANE)
    texts = exchange(jnp.broadcast_to(units[1], (n_text, part_rows, dim)), PLANE)
    texts = texts.reshape(n_text * part_rows, dim)
    images, texts = gather_ring(units[0], texts)
    factor = loss_scale * logit_scale / tokens_all
    scalars = jnp.stack([logit_scale, logit_bias, factor]).astype(F32)
    first = jnp.stack([lax.axis_index("c"), lax.axis_index(PLANE)]).astype(jnp.int32) * part_rows
    chip_part, fetched_part, other_part, text_part = loss_block(
        scalars, first, images, texts, part_rows
    )
    text_part = exchange(text_part.reshape(n_text, part_rows, dim), PLANE)
    image_grad, text_part = sum_ring(chip_part, fetched_part, other_part, text_part)
    text_grad = jnp.sum(text_part.astype(F32), axis=0)

    block_own = through_normalise(jnp.stack([image_grad, text_grad]), units, lengths)
    block_own = as_lies(block_own)
    block_low = as_lies(swap_join(as_lies(swap_join(block_own, "xh", 1)), "c", 1))
    hidden_grad = jnp.einsum("kte,kfe->ktf", block_low, fc2, preferred_element_type=F32)
    _, gelu_back = jax.vjp(gelu_tanh, preact)
    preact_grad = lax.optimization_barrier(gelu_back(hidden_grad)[0].astype(BF))
    normed_grad = jnp.einsum("ktf,kdf->ktd", preact_grad, fc1, preferred_element_type=F32)
    scaled = normed_grad * gains
    norm_term = (
        scaled
        - jnp.mean(scaled, axis=-1, keepdims=True)
        - standard * jnp.mean(scaled * standard, axis=-1, keepdims=True)
    ) * inverse
    norm_parts = as_lies(jnp.swapaxes(norm_term, 1, 2)).reshape(2, 2, 2, width, rows)
    norm_parts = as_lies(swap_sum(norm_parts, "c", 2))
    norm_share = as_lies(swap_sum(norm_parts, "xh", 1))
    block_share = as_lies(lax.dynamic_slice_in_dim(block_low, member * width, width, 2))
    block_share = as_lies(jnp.swapaxes(block_share, 1, 2)).astype(F32)
    return jnp.swapaxes(as_lies((block_share + norm_share).astype(BF)), 1, 2)


def solution(mesh):
    fine = Mesh(mesh.devices.reshape(4, 8, 2, 2, 2), ("y", "z", "xl", "xh", "c"))
    in_specs = (
        P(None, DP, TENSOR),
        P(),
        P(),
        P(None, None, TENSOR),
        P(None, TENSOR),
        P(None, TENSOR, None),
        P(),
        P(),
        P(),
        P(),
    )
    return jax.shard_map(
        on_device, mesh=fine, in_specs=in_specs, out_specs=P(None, DP, TENSOR), check_vma=False
    )
```

```python
import functools

import jax
import jax.numpy as jnp
from jax import lax
from jax.experimental import pallas as pl
from jax.experimental.layout import Layout, with_layout_constraint
from jax.experimental.pallas import tpu as pltpu
from jax.sharding import Mesh
from jax.sharding import PartitionSpec as P

TENSOR = ("xh", "c")
DP = ("y", "z", "xl")
PLANE = ("y", "xl", "xh")
BF = jnp.bfloat16
F32 = jnp.float32


def layer_stats(inputs):
    centred = inputs - jnp.mean(inputs, axis=-1, keepdims=True)
    inverse = lax.rsqrt(jnp.mean(centred * centred, axis=-1, keepdims=True) + 1e-06)
    return (centred * inverse, inverse)


def gelu_tanh(values):
    return jax.nn.gelu(values, approximate=True)


def normalise(blocks):
    lengths = jnp.sqrt(jnp.sum(blocks * blocks, axis=-1, keepdims=True) + 1e-06)
    return (as_lies((blocks / lengths).astype(BF)), lengths)


def through_normalise(unit_grad, units, lengths):
    unit_grad = as_lies(unit_grad)
    units = units.astype(F32)
    along = jnp.sum(units * unit_grad, axis=-1, keepdims=True)
    return ((unit_grad - units * along) / lengths).astype(BF)


def as_lies(array):
    return with_layout_constraint(array, Layout(tuple(range(array.ndim))))


def hop(block, places):
    size = lax.axis_size("z")
    pairs = [
        ((z + (places, -places)[core]) % size * 2 + core, z * 2 + core)
        for z in range(size)
        for core in range(2)
    ]
    return as_lies(lax.ppermute(as_lies(block), ("z", "c"), pairs))


def exchange(parts, axes):
    return lax.all_to_all(parts, axes, 0, 0, tiled=True)


def swap(block, axis):
    return as_lies(lax.ppermute(as_lies(block), axis, [(0, 1), (1, 0)]))


def pick(array, index, axis):
    return lax.dynamic_index_in_dim(array, index, axis, keepdims=False)


def swap_sum(parts, name, axis):
    me = lax.axis_index(name)
    got = swap(pick(parts, 1 - me, axis).astype(BF), name)
    return pick(parts, me, axis).astype(F32) + got.astype(F32)


def in_order(own, other, name, axis):
    first = lax.axis_index(name) == 0
    return jnp.concatenate(
        [jnp.where(first, own, other), jnp.where(first, other, own)], axis=axis
    )


def swap_join(own, name, axis):
    return in_order(own, swap(own, name), name, axis)


def gather_ring(own, texts):
    half = own.shape[0]
    chip = swap_join(own, "c", 0)
    one, two = hop(chip, 1), hop(chip, 2)
    three = hop(two, 1)
    four = hop(lax.dynamic_slice_in_dim(two, lax.axis_index("c") * half, half, 0), 2)
    fetched = jnp.concatenate([one, two, three, four], axis=0)
    fetched, texts = lax.optimization_barrier((fetched, texts))
    return jnp.concatenate([chip, fetched, swap(fetched, "c")], axis=0), texts


def sum_ring(chip, fetched, other, texts):
    half = chip.shape[0] // 2
    fetched = fetched.astype(F32) + swap(other, "c").astype(F32)
    one, two, three, four = jnp.split(fetched, [2 * half, 4 * half, 6 * half], axis=0)
    three = hop(three.astype(BF), -1).astype(F32)
    four = hop(four.astype(BF), -2)
    one, four = lax.optimization_barrier((one.astype(BF), four))
    one = hop(one, -1).astype(F32)
    four = four.astype(F32)
    first = lax.axis_index("c") == 0
    none = jnp.zeros_like(four)
    two = two + three
    two = two + jnp.concatenate([jnp.where(first, four, none), jnp.where(first, none, four)])
    two = hop(two.astype(BF), -2).astype(F32)
    own, texts = lax.optimization_barrier((chip + one + two, texts))
    return swap_sum(own.reshape(2, half, -1), "c", 0), texts


def loss_kernel(part_rows, scalars, first, images, texts, chip, fetched, other, text_part):
    scores = lax.dot_general(
        images[...], texts[...], (((1,), (1,)), ((), ())), preferred_element_type=F32
    )
    logits = scalars[0] * scores + scalars[1]
    at_image = lax.broadcasted_iota(jnp.int32, scores.shape, 0) - first[0]
    at_text = lax.broadcasted_iota(jnp.int32, scores.shape, 1) - first[1]
    diagonal = (at_image == at_text) & (at_image >= 0) & (at_image < part_rows)
    weights = (scalars[2] * (jax.nn.sigmoid(logits) - diagonal.astype(F32))).astype(BF)
    text_part[...] = lax.dot_general(
        weights, images[...], (((0,), (0,)), ((), ())), preferred_element_type=F32
    ).astype(BF)
    image_part = jnp.dot(weights, texts[...], preferred_element_type=F32)
    at_fetched, at_other = chip.shape[0], chip.shape[0] + fetched.shape[0]
    chip[...] = image_part[:at_fetched, :]
    fetched[...] = image_part[at_fetched:at_other, :].astype(BF)
    other[...] = image_part[at_other:, :].astype(BF)


def loss_block(scalars, first, images, texts, part_rows):
    rows, dim = images.shape
    fetched = rows // 2 - part_rows
    whole = pl.BlockSpec(memory_space=pltpu.VMEM)
    small = pl.BlockSpec(memory_space=pltpu.SMEM)
    return pl.pallas_call(
        functools.partial(loss_kernel, part_rows),
        in_specs=[small, small, whole, whole],
        out_specs=[whole] * 4,
        out_shape=[
            jax.ShapeDtypeStruct((2 * part_rows, dim), F32),
            jax.ShapeDtypeStruct((fetched, dim), BF),
            jax.ShapeDtypeStruct((fetched, dim), BF),
            jax.ShapeDtypeStruct(texts.shape, BF),
        ],
        compiler_params=pltpu.CompilerParams(vmem_limit_bytes=20 * 1024 * 1024),
        cost_estimate=pl.CostEstimate(
            flops=6 * rows * texts.shape[0] * dim,
            bytes_accessed=10 * rows * dim,
            transcendentals=rows * texts.shape[0],
        ),
    )(scalars, first, images, texts)


def on_device(
    pooled, ln_gain, ln_bias, fc1, fc1_bias, fc2, fc2_bias, logit_scale, logit_bias, loss_scale
):
    rows, width = pooled.shape[1], pooled.shape[2]
    member = lax.axis_index(TENSOR)
    part_rows = rows // lax.axis_size(TENSOR)
    tokens_all = rows * lax.axis_size(DP)

    own = jnp.swapaxes(pooled, 1, 2)
    far = swap(own, "xh")
    none = jnp.zeros_like(own)
    mine = in_order(own[:, None, None], none[:, None, None], "xh", 1)
    far, mine = lax.optimization_barrier((far, mine))
    whole = mine + in_order(none[:, None, None], far[:, None, None], "xh", 1)
    whole = swap_join(whole, "c", 2).reshape(2, 4 * width, rows)
    whole, ln_gain, ln_bias, fc1_bias, fc2_bias = lax.optimization_barrier(
        (whole, ln_gain, ln_bias, fc1_bias, fc2_bias)
    )
    inputs = jnp.swapaxes(whole, 1, 2).astype(F32)
    dim = inputs.shape[2]
    standard, inverse = layer_stats(inputs)
    gains = ln_gain.astype(F32)[:, None, :]
    normed = (standard * gains + ln_bias.astype(F32)[:, None, :]).astype(BF)
    preact = jnp.einsum("ktd,kdf->ktf", normed, fc1, preferred_element_type=F32)
    preact = preact + fc1_bias.astype(F32)[:, None, :]
    hidden = gelu_tanh(preact).astype(BF)
    partial = as_lies(jnp.einsum("ktf,kfe->kte", hidden, fc2, preferred_element_type=F32))

    quarter = lax.axis_index("c") * 2 + lax.axis_index("xh")
    partial = swap_sum(partial.reshape(2, 2, 2 * part_rows, dim), "c", 1)
    summed = swap_sum(partial.reshape(2, 2, part_rows, dim), "xh", 1)
    own_inputs = as_lies(lax.dynamic_slice_in_dim(inputs, quarter * part_rows, part_rows, 1))
    units, lengths = normalise(own_inputs + summed + fc2_bias.astype(F32)[:, None, :])

    n_text = lax.axis_size(PLANE)
    texts = exchange(jnp.broadcast_to(units[1], (n_text, part_rows, dim)), PLANE)
    texts = texts.reshape(n_text * part_rows, dim)
    images, texts = gather_ring(units[0], texts)
    factor = loss_scale * logit_scale / tokens_all
    scalars = jnp.stack([logit_scale, logit_bias, factor]).astype(F32)
    first = jnp.stack([lax.axis_index("c"), lax.axis_index(PLANE)]).astype(jnp.int32) * part_rows
    chip_part, fetched_part, other_part, text_part = loss_block(
        scalars, first, images, texts, part_rows
    )
    text_part = exchange(text_part.reshape(n_text, part_rows, dim), PLANE)
    image_grad, text_part = sum_ring(chip_part, fetched_part, other_part, text_part)
    text_grad = jnp.sum(text_part.astype(F32), axis=0)

    block_own = through_normalise(jnp.stack([image_grad, text_grad]), units, lengths)
    block_own = as_lies(block_own)
    block_own, preact = lax.optimization_barrier((block_own, preact))
    far = swap(block_own, "xh")
    _, gelu_back = jax.vjp(gelu_tanh, preact)
    slope = gelu_back(jnp.ones_like(preact))[0]
    far, slope = lax.optimization_barrier((far, slope))
    block_low = as_lies(in_order(block_own, far, "xh", 1))
    block_low = as_lies(swap_join(block_low, "c", 1))
    hidden_grad = jnp.einsum("kte,kfe->ktf", block_low, fc2, preferred_element_type=F32)
    preact_grad = lax.optimization_barrier((hidden_grad * slope).astype(BF))
    normed_grad = jnp.einsum("ktf,kdf->ktd", preact_grad, fc1, preferred_element_type=F32)
    scaled = normed_grad * gains
    norm_term = (
        scaled
        - jnp.mean(scaled, axis=-1, keepdims=True)
        - standard * jnp.mean(scaled * standard, axis=-1, keepdims=True)
    ) * inverse
    norm_parts = as_lies(jnp.swapaxes(norm_term, 1, 2)).reshape(2, 2, 2, width, rows)
    norm_parts = as_lies(swap_sum(norm_parts, "c", 2))
    norm_share = as_lies(swap_sum(norm_parts, "xh", 1))
    block_share = as_lies(lax.dynamic_slice_in_dim(block_low, member * width, width, 2))
    block_share = as_lies(jnp.swapaxes(block_share, 1, 2)).astype(F32)
    return jnp.swapaxes(as_lies((block_share + norm_share).astype(BF)), 1, 2)


def solution(mesh):
    fine = Mesh(mesh.devices.reshape(4, 8, 2, 2, 2), ("y", "z", "xl", "xh", "c"))
    in_specs = (
        P(None, DP, TENSOR),
        P(),
        P(),
        P(None, None, TENSOR),
        P(None, TENSOR),
        P(None, TENSOR, None),
        P(),
        P(),
        P(),
        P(),
    )
    return jax.shard_map(
        on_device, mesh=fine, in_specs=in_specs, out_specs=P(None, DP, TENSOR), check_vma=False
    )
```

```python
import functools

import jax
import jax.numpy as jnp
from jax import lax
from jax.experimental import pallas as pl
from jax.experimental.layout import Layout, with_layout_constraint
from jax.experimental.pallas import tpu as pltpu
from jax.sharding import Mesh
from jax.sharding import PartitionSpec as P

TENSOR = ("xh", "c")
DP = ("y", "z", "xl")
PLANE = ("y", "xl", "xh")
BF = jnp.bfloat16
F32 = jnp.float32


def layer_stats(inputs):
    centred = inputs - jnp.mean(inputs, axis=-1, keepdims=True)
    inverse = lax.rsqrt(jnp.mean(centred * centred, axis=-1, keepdims=True) + 1e-06)
    return (centred * inverse, inverse)


def gelu_tanh(values):
    return jax.nn.gelu(values, approximate=True)


def normalise(blocks):
    lengths = jnp.sqrt(jnp.sum(blocks * blocks, axis=-1, keepdims=True) + 1e-06)
    return (as_lies((blocks / lengths).astype(BF)), lengths)


def through_normalise(unit_grad, units, lengths):
    unit_grad = as_lies(unit_grad)
    units = units.astype(F32)
    along = jnp.sum(units * unit_grad, axis=-1, keepdims=True)
    return ((unit_grad - units * along) / lengths).astype(BF)


def as_lies(array):
    return with_layout_constraint(array, Layout(tuple(range(array.ndim))))


def hop(block, places):
    size = lax.axis_size("z")
    pairs = [
        ((z + (places, -places)[core]) % size * 2 + core, z * 2 + core)
        for z in range(size)
        for core in range(2)
    ]
    return as_lies(lax.ppermute(as_lies(block), ("z", "c"), pairs))


def exchange(parts, axes):
    return lax.all_to_all(parts, axes, 0, 0, tiled=True)


def swap(block, axis):
    return as_lies(lax.ppermute(as_lies(block), axis, [(0, 1), (1, 0)]))


def pick(array, index, axis):
    return lax.dynamic_index_in_dim(array, index, axis, keepdims=False)


def swap_sum(parts, name, axis):
    me = lax.axis_index(name)
    got = swap(pick(parts, 1 - me, axis).astype(BF), name)
    return pick(parts, me, axis).astype(F32) + got.astype(F32)


def in_order(own, other, name, axis):
    first = lax.axis_index(name) == 0
    return jnp.concatenate(
        [jnp.where(first, own, other), jnp.where(first, other, own)], axis=axis
    )


def swap_join(own, name, axis):
    return in_order(own, swap(own, name), name, axis)


def gather_ring(own, texts):
    half = own.shape[0]
    chip = swap_join(own, "c", 0)
    one, two = hop(chip, 1), hop(chip, 2)
    three = hop(two, 1)
    four = hop(lax.dynamic_slice_in_dim(two, lax.axis_index("c") * half, half, 0), 2)
    fetched = jnp.concatenate([one, two, three, four], axis=0)
    fetched, texts = lax.optimization_barrier((fetched, texts))
    return jnp.concatenate([chip, fetched, swap(fetched, "c")], axis=0), texts


def sum_ring(chip, fetched, other, texts):
    half = chip.shape[0] // 2
    fetched = fetched.astype(F32) + swap(other, "c").astype(F32)
    one, two, three, four = jnp.split(fetched, [2 * half, 4 * half, 6 * half], axis=0)
    three = hop(three.astype(BF), -1).astype(F32)
    four = hop(four.astype(BF), -2).astype(F32)
    first = lax.axis_index("c") == 0
    none = jnp.zeros_like(four)
    two = two + three
    two = two + jnp.concatenate([jnp.where(first, four, none), jnp.where(first, none, four)])
    two, one = lax.optimization_barrier((two.astype(BF), one.astype(BF)))
    two = hop(two, -2).astype(F32)
    one = hop(one, -1).astype(F32)
    own, texts = lax.optimization_barrier((chip + one + two, texts))
    return swap_sum(own.reshape(2, half, -1), "c", 0), texts


def loss_kernel(part_rows, scalars, first, images, texts, chip, fetched, other, text_part):
    scores = lax.dot_general(
        images[...], texts[...], (((1,), (1,)), ((), ())), preferred_element_type=F32
    )
    logits = scalars[0] * scores + scalars[1]
    at_image = lax.broadcasted_iota(jnp.int32, scores.shape, 0) - first[0]
    at_text = lax.broadcasted_iota(jnp.int32, scores.shape, 1) - first[1]
    diagonal = (at_image == at_text) & (at_image >= 0) & (at_image < part_rows)
    weights = (scalars[2] * (jax.nn.sigmoid(logits) - diagonal.astype(F32))).astype(BF)
    text_part[...] = lax.dot_general(
        weights, images[...], (((0,), (0,)), ((), ())), preferred_element_type=F32
    ).astype(BF)
    image_part = jnp.dot(weights, texts[...], preferred_element_type=F32)
    at_fetched, at_other = chip.shape[0], chip.shape[0] + fetched.shape[0]
    chip[...] = image_part[:at_fetched, :]
    fetched[...] = image_part[at_fetched:at_other, :].astype(BF)
    other[...] = image_part[at_other:, :].astype(BF)


def loss_block(scalars, first, images, texts, part_rows):
    rows, dim = images.shape
    fetched = rows // 2 - part_rows
    whole = pl.BlockSpec(memory_space=pltpu.VMEM)
    small = pl.BlockSpec(memory_space=pltpu.SMEM)
    return pl.pallas_call(
        functools.partial(loss_kernel, part_rows),
        in_specs=[small, small, whole, whole],
        out_specs=[whole] * 4,
        out_shape=[
            jax.ShapeDtypeStruct((2 * part_rows, dim), F32),
            jax.ShapeDtypeStruct((fetched, dim), BF),
            jax.ShapeDtypeStruct((fetched, dim), BF),
            jax.ShapeDtypeStruct(texts.shape, BF),
        ],
        compiler_params=pltpu.CompilerParams(vmem_limit_bytes=20 * 1024 * 1024),
        cost_estimate=pl.CostEstimate(
            flops=6 * rows * texts.shape[0] * dim,
            bytes_accessed=10 * rows * dim,
            transcendentals=rows * texts.shape[0],
        ),
    )(scalars, first, images, texts)


def on_device(
    pooled, ln_gain, ln_bias, fc1, fc1_bias, fc2, fc2_bias, logit_scale, logit_bias, loss_scale
):
    rows, width = pooled.shape[1], pooled.shape[2]
    member = lax.axis_index(TENSOR)
    part_rows = rows // lax.axis_size(TENSOR)
    tokens_all = rows * lax.axis_size(DP)

    own = jnp.swapaxes(pooled, 1, 2)
    far = swap(own, "xh")
    none = jnp.zeros_like(own)
    mine = in_order(own[:, None, None], none[:, None, None], "xh", 1)
    far, mine = lax.optimization_barrier((far, mine))
    whole = mine + in_order(none[:, None, None], far[:, None, None], "xh", 1)
    whole = swap_join(whole, "c", 2).reshape(2, 4 * width, rows)
    whole, ln_gain, ln_bias, fc1_bias, fc2_bias = lax.optimization_barrier(
        (whole, ln_gain, ln_bias, fc1_bias, fc2_bias)
    )
    inputs = jnp.swapaxes(whole, 1, 2).astype(F32)
    dim = inputs.shape[2]
    standard, inverse = layer_stats(inputs)
    gains = ln_gain.astype(F32)[:, None, :]
    normed = (standard * gains + ln_bias.astype(F32)[:, None, :]).astype(BF)
    preact = jnp.einsum("ktd,kdf->ktf", normed, fc1, preferred_element_type=F32)
    preact = preact + fc1_bias.astype(F32)[:, None, :]
    hidden = gelu_tanh(preact).astype(BF)
    partial = as_lies(jnp.einsum("ktf,kfe->kte", hidden, fc2, preferred_element_type=F32))

    quarter = lax.axis_index("c") * 2 + lax.axis_index("xh")
    partial = swap_sum(partial.reshape(2, 2, 2 * part_rows, dim), "c", 1)
    summed = swap_sum(partial.reshape(2, 2, part_rows, dim), "xh", 1)
    own_inputs = as_lies(lax.dynamic_slice_in_dim(inputs, quarter * part_rows, part_rows, 1))
    units, lengths = normalise(own_inputs + summed + fc2_bias.astype(F32)[:, None, :])

    n_text = lax.axis_size(PLANE)
    texts = exchange(jnp.broadcast_to(units[1], (n_text, part_rows, dim)), PLANE)
    texts = texts.reshape(n_text * part_rows, dim)
    images, texts = gather_ring(units[0], texts)
    factor = loss_scale * logit_scale / tokens_all
    scalars = jnp.stack([logit_scale, logit_bias, factor]).astype(F32)
    first = jnp.stack([lax.axis_index("c"), lax.axis_index(PLANE)]).astype(jnp.int32) * part_rows
    chip_part, fetched_part, other_part, text_part = loss_block(
        scalars, first, images, texts, part_rows
    )
    text_part = exchange(text_part.reshape(n_text, part_rows, dim), PLANE)
    image_grad, text_part = sum_ring(chip_part, fetched_part, other_part, text_part)
    text_grad = jnp.sum(text_part.astype(F32), axis=0)

    block_own = through_normalise(jnp.stack([image_grad, text_grad]), units, lengths)
    block_own = as_lies(block_own)
    block_own, preact = lax.optimization_barrier((block_own, preact))
    far = swap(block_own, "xh")
    _, gelu_back = jax.vjp(gelu_tanh, preact)
    slope = gelu_back(jnp.ones_like(preact))[0]
    far, slope = lax.optimization_barrier((far, slope))
    block_low = as_lies(in_order(block_own, far, "xh", 1))
    block_low = as_lies(swap_join(block_low, "c", 1))
    hidden_grad = jnp.einsum("kte,kfe->ktf", block_low, fc2, preferred_element_type=F32)
    preact_grad = lax.optimization_barrier((hidden_grad * slope).astype(BF))
    normed_grad = jnp.einsum("ktf,kdf->ktd", preact_grad, fc1, preferred_element_type=F32)
    scaled = normed_grad * gains
    norm_term = (
        scaled
        - jnp.mean(scaled, axis=-1, keepdims=True)
        - standard * jnp.mean(scaled * standard, axis=-1, keepdims=True)
    ) * inverse
    norm_parts = as_lies(jnp.swapaxes(norm_term, 1, 2)).reshape(2, 2, 2, width, rows)
    norm_parts = as_lies(swap_sum(norm_parts, "c", 2))
    norm_share = as_lies(swap_sum(norm_parts, "xh", 1))
    block_share = as_lies(lax.dynamic_slice_in_dim(block_low, member * width, width, 2))
    block_share = as_lies(jnp.swapaxes(block_share, 1, 2)).astype(F32)
    return jnp.swapaxes(as_lies((block_share + norm_share).astype(BF)), 1, 2)


def solution(mesh):
    fine = Mesh(mesh.devices.reshape(4, 8, 2, 2, 2), ("y", "z", "xl", "xh", "c"))
    in_specs = (
        P(None, DP, TENSOR),
        P(),
        P(),
        P(None, None, TENSOR),
        P(None, TENSOR),
        P(None, TENSOR, None),
        P(),
        P(),
        P(),
        P(),
    )
    return jax.shard_map(
        on_device, mesh=fine, in_specs=in_specs, out_specs=P(None, DP, TENSOR), check_vma=False
    )
```

```python
import functools

import jax
import jax.numpy as jnp
from jax import lax
from jax.experimental import pallas as pl
from jax.experimental.layout import Layout, with_layout_constraint
from jax.experimental.pallas import tpu as pltpu
from jax.sharding import Mesh
from jax.sharding import PartitionSpec as P

TENSOR = ("xh", "c")
DP = ("y", "z", "xl")
PLANE = ("y", "xl", "xh")
BF = jnp.bfloat16
F32 = jnp.float32


def layer_stats(inputs):
    centred = inputs - jnp.mean(inputs, axis=-1, keepdims=True)
    inverse = lax.rsqrt(jnp.mean(centred * centred, axis=-1, keepdims=True) + 1e-06)
    return (centred * inverse, inverse)


def gelu_tanh(values):
    return jax.nn.gelu(values, approximate=True)


def normalise(blocks):
    lengths = jnp.sqrt(jnp.sum(blocks * blocks, axis=-1, keepdims=True) + 1e-06)
    return (as_lies((blocks / lengths).astype(BF)), lengths)


def through_normalise(unit_grad, units, lengths):
    unit_grad = as_lies(unit_grad)
    units = units.astype(F32)
    along = jnp.sum(units * unit_grad, axis=-1, keepdims=True)
    return ((unit_grad - units * along) / lengths).astype(BF)


def as_lies(array):
    return with_layout_constraint(array, Layout(tuple(range(array.ndim))))


def hop(block, places):
    size = lax.axis_size("z")
    pairs = [
        ((z + (places, -places)[core]) % size * 2 + core, z * 2 + core)
        for z in range(size)
        for core in range(2)
    ]
    return as_lies(lax.ppermute(as_lies(block), ("z", "c"), pairs))


def exchange(parts, axes):
    return lax.all_to_all(parts, axes, 0, 0, tiled=True)


def swap(block, axis):
    return as_lies(lax.ppermute(as_lies(block), axis, [(0, 1), (1, 0)]))


def pick(array, index, axis):
    return lax.dynamic_index_in_dim(array, index, axis, keepdims=False)


def swap_sum(parts, name, axis):
    me = lax.axis_index(name)
    got = swap(pick(parts, 1 - me, axis).astype(BF), name)
    return pick(parts, me, axis).astype(F32) + got.astype(F32)


def in_order(own, other, name, axis):
    first = lax.axis_index(name) == 0
    return jnp.concatenate(
        [jnp.where(first, own, other), jnp.where(first, other, own)], axis=axis
    )


def swap_join(own, name, axis):
    return in_order(own, swap(own, name), name, axis)


def gather_ring(own, texts):
    chip = swap_join(own, "c", 0)
    one, two = hop(chip, 1), hop(chip, 2)
    three = hop(two, 1)
    four = hop(own, 4)
    fetched = jnp.concatenate([one, two, three, four], axis=0)
    fetched, texts = lax.optimization_barrier((fetched, texts))
    return jnp.concatenate([chip, fetched, swap(fetched, "c")], axis=0), texts


def sum_ring(chip, fetched, other, texts):
    half = chip.shape[0] // 2
    fetched = fetched.astype(F32) + swap(other, "c").astype(F32)
    one, two, three, four = jnp.split(fetched, [2 * half, 4 * half, 6 * half], axis=0)
    three = hop(three.astype(BF), -1).astype(F32)
    four = hop(four.astype(BF), -2)
    one, four = lax.optimization_barrier((one.astype(BF), four))
    one = hop(one, -1).astype(F32)
    four = four.astype(F32)
    first = lax.axis_index("c") == 0
    none = jnp.zeros_like(four)
    two = two + three
    two = two + jnp.concatenate([jnp.where(first, four, none), jnp.where(first, none, four)])
    two = hop(two.astype(BF), -2).astype(F32)
    own, texts = lax.optimization_barrier((chip + one + two, texts))
    return swap_sum(own.reshape(2, half, -1), "c", 0), texts


def loss_kernel(part_rows, scalars, first, images, texts, chip, fetched, other, text_part):
    scores = lax.dot_general(
        images[...], texts[...], (((1,), (1,)), ((), ())), preferred_element_type=F32
    )
    logits = scalars[0] * scores + scalars[1]
    at_image = lax.broadcasted_iota(jnp.int32, scores.shape, 0) - first[0]
    at_text = lax.broadcasted_iota(jnp.int32, scores.shape, 1) - first[1]
    diagonal = (at_image == at_text) & (at_image >= 0) & (at_image < part_rows)
    weights = (scalars[2] * (jax.nn.sigmoid(logits) - diagonal.astype(F32))).astype(BF)
    text_part[...] = lax.dot_general(
        weights, images[...], (((0,), (0,)), ((), ())), preferred_element_type=F32
    ).astype(BF)
    image_part = jnp.dot(weights, texts[...], preferred_element_type=F32)
    at_fetched, at_other = chip.shape[0], chip.shape[0] + fetched.shape[0]
    chip[...] = image_part[:at_fetched, :]
    fetched[...] = image_part[at_fetched:at_other, :].astype(BF)
    other[...] = image_part[at_other:, :].astype(BF)


def loss_block(scalars, first, images, texts, part_rows):
    rows, dim = images.shape
    fetched = rows // 2 - part_rows
    whole = pl.BlockSpec(memory_space=pltpu.VMEM)
    small = pl.BlockSpec(memory_space=pltpu.SMEM)
    return pl.pallas_call(
        functools.partial(loss_kernel, part_rows),
        in_specs=[small, small, whole, whole],
        out_specs=[whole] * 4,
        out_shape=[
            jax.ShapeDtypeStruct((2 * part_rows, dim), F32),
            jax.ShapeDtypeStruct((fetched, dim), BF),
            jax.ShapeDtypeStruct((fetched, dim), BF),
            jax.ShapeDtypeStruct(texts.shape, BF),
        ],
        compiler_params=pltpu.CompilerParams(vmem_limit_bytes=20 * 1024 * 1024),
        cost_estimate=pl.CostEstimate(
            flops=6 * rows * texts.shape[0] * dim,
            bytes_accessed=10 * rows * dim,
            transcendentals=rows * texts.shape[0],
        ),
    )(scalars, first, images, texts)


def on_device(
    pooled, ln_gain, ln_bias, fc1, fc1_bias, fc2, fc2_bias, logit_scale, logit_bias, loss_scale
):
    rows, width = pooled.shape[1], pooled.shape[2]
    member = lax.axis_index(TENSOR)
    part_rows = rows // lax.axis_size(TENSOR)
    tokens_all = rows * lax.axis_size(DP)

    own = jnp.swapaxes(pooled, 1, 2)
    far = swap(own, "xh")
    none = jnp.zeros_like(own)
    mine = in_order(own[:, None, None], none[:, None, None], "xh", 1)
    far, mine = lax.optimization_barrier((far, mine))
    whole = mine + in_order(none[:, None, None], far[:, None, None], "xh", 1)
    whole = swap_join(whole, "c", 2).reshape(2, 4 * width, rows)
    whole, ln_gain, ln_bias, fc1_bias, fc2_bias = lax.optimization_barrier(
        (whole, ln_gain, ln_bias, fc1_bias, fc2_bias)
    )
    inputs = jnp.swapaxes(whole, 1, 2).astype(F32)
    dim = inputs.shape[2]
    standard, inverse = layer_stats(inputs)
    gains = ln_gain.astype(F32)[:, None, :]
    normed = (standard * gains + ln_bias.astype(F32)[:, None, :]).astype(BF)
    preact = jnp.einsum("ktd,kdf->ktf", normed, fc1, preferred_element_type=F32)
    preact = preact + fc1_bias.astype(F32)[:, None, :]
    hidden = gelu_tanh(preact).astype(BF)
    partial = as_lies(jnp.einsum("ktf,kfe->kte", hidden, fc2, preferred_element_type=F32))

    quarter = lax.axis_index("c") * 2 + lax.axis_index("xh")
    partial = swap_sum(partial.reshape(2, 2, 2 * part_rows, dim), "c", 1)
    summed = swap_sum(partial.reshape(2, 2, part_rows, dim), "xh", 1)
    own_inputs = as_lies(lax.dynamic_slice_in_dim(inputs, quarter * part_rows, part_rows, 1))
    units, lengths = normalise(own_inputs + summed + fc2_bias.astype(F32)[:, None, :])

    n_text = lax.axis_size(PLANE)
    texts = exchange(jnp.broadcast_to(units[1], (n_text, part_rows, dim)), PLANE)
    texts = texts.reshape(n_text * part_rows, dim)
    images, texts = gather_ring(units[0], texts)
    factor = loss_scale * logit_scale / tokens_all
    scalars = jnp.stack([logit_scale, logit_bias, factor]).astype(F32)
    first = jnp.stack([lax.axis_index("c"), lax.axis_index(PLANE)]).astype(jnp.int32) * part_rows
    chip_part, fetched_part, other_part, text_part = loss_block(
        scalars, first, images, texts, part_rows
    )
    text_part = exchange(text_part.reshape(n_text, part_rows, dim), PLANE)
    image_grad, text_part = sum_ring(chip_part, fetched_part, other_part, text_part)
    text_grad = jnp.sum(text_part.astype(F32), axis=0)

    block_own = through_normalise(jnp.stack([image_grad, text_grad]), units, lengths)
    block_own = as_lies(block_own)
    block_own, preact = lax.optimization_barrier((block_own, preact))
    far = swap(block_own, "xh")
    _, gelu_back = jax.vjp(gelu_tanh, preact)
    slope = gelu_back(jnp.ones_like(preact))[0]
    far, slope = lax.optimization_barrier((far, slope))
    block_low = as_lies(in_order(block_own, far, "xh", 1))
    block_low = as_lies(swap_join(block_low, "c", 1))
    hidden_grad = jnp.einsum("kte,kfe->ktf", block_low, fc2, preferred_element_type=F32)
    preact_grad = lax.optimization_barrier((hidden_grad * slope).astype(BF))
    normed_grad = jnp.einsum("ktf,kdf->ktd", preact_grad, fc1, preferred_element_type=F32)
    scaled = normed_grad * gains
    norm_term = (
        scaled
        - jnp.mean(scaled, axis=-1, keepdims=True)
        - standard * jnp.mean(scaled * standard, axis=-1, keepdims=True)
    ) * inverse
    norm_parts = as_lies(jnp.swapaxes(norm_term, 1, 2)).reshape(2, 2, 2, width, rows)
    norm_parts = as_lies(swap_sum(norm_parts, "c", 2))
    norm_share = as_lies(swap_sum(norm_parts, "xh", 1))
    block_share = as_lies(lax.dynamic_slice_in_dim(block_low, member * width, width, 2))
    block_share = as_lies(jnp.swapaxes(block_share, 1, 2)).astype(F32)
    return jnp.swapaxes(as_lies((block_share + norm_share).astype(BF)), 1, 2)


def solution(mesh):
    fine = Mesh(mesh.devices.reshape(4, 8, 2, 2, 2), ("y", "z", "xl", "xh", "c"))
    in_specs = (
        P(None, DP, TENSOR),
        P(),
        P(),
        P(None, None, TENSOR),
        P(None, TENSOR),
        P(None, TENSOR, None),
        P(),
        P(),
        P(),
        P(),
    )
    return jax.shard_map(
        on_device, mesh=fine, in_specs=in_specs, out_specs=P(None, DP, TENSOR), check_vma=False
    )
```

```python
import functools

import jax
import jax.numpy as jnp
from jax import lax
from jax.experimental import pallas as pl
from jax.experimental.layout import Layout, with_layout_constraint
from jax.experimental.pallas import tpu as pltpu
from jax.sharding import Mesh
from jax.sharding import PartitionSpec as P

TENSOR = ("xh", "c")
DP = ("y", "z", "xl")
PLANE = ("y", "xl", "xh")
BF = jnp.bfloat16
F32 = jnp.float32


def layer_stats(inputs):
    centred = inputs - jnp.mean(inputs, axis=-1, keepdims=True)
    inverse = lax.rsqrt(jnp.mean(centred * centred, axis=-1, keepdims=True) + 1e-06)
    return (centred * inverse, inverse)


def gelu_tanh(values):
    return jax.nn.gelu(values, approximate=True)


def normalise(blocks):
    lengths = jnp.sqrt(jnp.sum(blocks * blocks, axis=-1, keepdims=True) + 1e-06)
    return (as_lies((blocks / lengths).astype(BF)), lengths)


def through_normalise(unit_grad, units, lengths):
    unit_grad = as_lies(unit_grad)
    units = units.astype(F32)
    along = jnp.sum(units * unit_grad, axis=-1, keepdims=True)
    return ((unit_grad - units * along) / lengths).astype(BF)


def as_lies(array):
    return with_layout_constraint(array, Layout(tuple(range(array.ndim))))


def hop(block, places):
    size = lax.axis_size("z")
    pairs = [
        ((z + (places, -places)[core]) % size * 2 + core, z * 2 + core)
        for z in range(size)
        for core in range(2)
    ]
    return as_lies(lax.ppermute(as_lies(block), ("z", "c"), pairs))


def exchange(parts, axes):
    return lax.all_to_all(parts, axes, 0, 0, tiled=True)


def swap(block, axis):
    return as_lies(lax.ppermute(as_lies(block), axis, [(0, 1), (1, 0)]))


def pick(array, index, axis):
    return lax.dynamic_index_in_dim(array, index, axis, keepdims=False)


def swap_sum(parts, name, axis):
    me = lax.axis_index(name)
    got = swap(pick(parts, 1 - me, axis).astype(BF), name)
    return pick(parts, me, axis).astype(F32) + got.astype(F32)


def in_order(own, other, name, axis):
    first = lax.axis_index(name) == 0
    return jnp.concatenate(
        [jnp.where(first, own, other), jnp.where(first, other, own)], axis=axis
    )


def swap_join(own, name, axis):
    return in_order(own, swap(own, name), name, axis)


def gather_ring(own, texts):
    half = own.shape[0]
    chip = swap_join(own, "c", 0)
    one, two = hop(chip, 1), hop(chip, 2)
    three = hop(two, 1)
    four = hop(lax.dynamic_slice_in_dim(two, lax.axis_index("c") * half, half, 0), 2)
    fetched = jnp.concatenate([one, two, three, four], axis=0)
    fetched, texts = lax.optimization_barrier((fetched, texts))
    return jnp.concatenate([chip, fetched, swap(fetched, "c")], axis=0), texts


def sum_ring(chip, fetched, other, texts):
    half = chip.shape[0] // 2
    fetched = fetched.astype(F32) + swap(other, "c").astype(F32)
    one, two, three, four = jnp.split(fetched, [2 * half, 4 * half, 6 * half], axis=0)
    three = hop(three.astype(BF), -1).astype(F32)
    four = hop(four.astype(BF), -2)
    one, four = lax.optimization_barrier((one.astype(BF), four))
    one = hop(one, -1).astype(F32)
    four = four.astype(F32)
    first = lax.axis_index("c") == 0
    none = jnp.zeros_like(four)
    two = two + three
    two = two + jnp.concatenate([jnp.where(first, four, none), jnp.where(first, none, four)])
    two = hop(two.astype(BF), -2).astype(F32)
    own, texts = lax.optimization_barrier((chip + one + two, texts))
    return swap_sum(own.reshape(2, half, -1), "c", 0), texts


def loss_kernel(part_rows, scalars, first, images, texts, chip, fetched, other, text_part):
    scores = lax.dot_general(
        images[...], texts[...], (((1,), (1,)), ((), ())), preferred_element_type=F32
    )
    logits = scalars[0] * scores + scalars[1]
    at_image = lax.broadcasted_iota(jnp.int32, scores.shape, 0) - first[0]
    at_text = lax.broadcasted_iota(jnp.int32, scores.shape, 1) - first[1]
    diagonal = (at_image == at_text) & (at_image >= 0) & (at_image < part_rows)
    weights = (scalars[2] * (jax.nn.sigmoid(logits) - diagonal.astype(F32))).astype(BF)
    text_part[...] = lax.dot_general(
        weights, images[...], (((0,), (0,)), ((), ())), preferred_element_type=F32
    ).astype(BF)
    image_part = jnp.dot(weights, texts[...], preferred_element_type=F32)
    at_fetched, at_other = chip.shape[0], chip.shape[0] + fetched.shape[0]
    chip[...] = image_part[:at_fetched, :]
    fetched[...] = image_part[at_fetched:at_other, :].astype(BF)
    other[...] = image_part[at_other:, :].astype(BF)


def loss_block(scalars, first, images, texts, part_rows):
    rows, dim = images.shape
    fetched = rows // 2 - part_rows
    whole = pl.BlockSpec(memory_space=pltpu.VMEM)
    small = pl.BlockSpec(memory_space=pltpu.SMEM)
    return pl.pallas_call(
        functools.partial(loss_kernel, part_rows),
        in_specs=[small, small, whole, whole],
        out_specs=[whole] * 4,
        out_shape=[
            jax.ShapeDtypeStruct((2 * part_rows, dim), F32),
            jax.ShapeDtypeStruct((fetched, dim), BF),
            jax.ShapeDtypeStruct((fetched, dim), BF),
            jax.ShapeDtypeStruct(texts.shape, BF),
        ],
        compiler_params=pltpu.CompilerParams(vmem_limit_bytes=20 * 1024 * 1024),
        cost_estimate=pl.CostEstimate(
            flops=6 * rows * texts.shape[0] * dim,
            bytes_accessed=10 * rows * dim,
            transcendentals=rows * texts.shape[0],
        ),
    )(scalars, first, images, texts)


def on_device(
    pooled, ln_gain, ln_bias, fc1, fc1_bias, fc2, fc2_bias, logit_scale, logit_bias, loss_scale
):
    rows, width = pooled.shape[1], pooled.shape[2]
    member = lax.axis_index(TENSOR)
    part_rows = rows // lax.axis_size(TENSOR)
    tokens_all = rows * lax.axis_size(DP)

    own = jnp.swapaxes(pooled, 1, 2)
    far = swap(own, "xh")
    none = jnp.zeros_like(own)
    mine = in_order(own[:, None, None], none[:, None, None], "xh", 1)
    far, mine = lax.optimization_barrier((far, mine))
    whole = mine + in_order(none[:, None, None], far[:, None, None], "xh", 1)
    whole = swap_join(whole, "c", 2).reshape(2, 4 * width, rows)
    whole, ln_gain, ln_bias, fc1_bias, fc2_bias = lax.optimization_barrier(
        (whole, ln_gain, ln_bias, fc1_bias, fc2_bias)
    )
    inputs = jnp.swapaxes(whole, 1, 2).astype(F32)
    dim = inputs.shape[2]
    standard, inverse = layer_stats(inputs)
    gains = ln_gain.astype(F32)[:, None, :]
    normed = (standard * gains + ln_bias.astype(F32)[:, None, :]).astype(BF)
    normed = lax.optimization_barrier(normed)
    preact = jnp.einsum("ktd,kdf->ktf", normed, fc1, preferred_element_type=F32)
    preact = preact + fc1_bias.astype(F32)[:, None, :]
    hidden = gelu_tanh(preact).astype(BF)
    partial = as_lies(jnp.einsum("ktf,kfe->kte", hidden, fc2, preferred_element_type=F32))

    quarter = lax.axis_index("c") * 2 + lax.axis_index("xh")
    partial = swap_sum(partial.reshape(2, 2, 2 * part_rows, dim), "c", 1)
    summed = swap_sum(partial.reshape(2, 2, part_rows, dim), "xh", 1)
    own_inputs = as_lies(lax.dynamic_slice_in_dim(inputs, quarter * part_rows, part_rows, 1))
    units, lengths = normalise(own_inputs + summed + fc2_bias.astype(F32)[:, None, :])

    n_text = lax.axis_size(PLANE)
    texts = exchange(jnp.broadcast_to(units[1], (n_text, part_rows, dim)), PLANE)
    texts = texts.reshape(n_text * part_rows, dim)
    images, texts = gather_ring(units[0], texts)
    factor = loss_scale * logit_scale / tokens_all
    scalars = jnp.stack([logit_scale, logit_bias, factor]).astype(F32)
    first = jnp.stack([lax.axis_index("c"), lax.axis_index(PLANE)]).astype(jnp.int32) * part_rows
    chip_part, fetched_part, other_part, text_part = loss_block(
        scalars, first, images, texts, part_rows
    )
    text_part = exchange(text_part.reshape(n_text, part_rows, dim), PLANE)
    image_grad, text_part = sum_ring(chip_part, fetched_part, other_part, text_part)
    text_grad = jnp.sum(text_part.astype(F32), axis=0)

    block_own = through_normalise(jnp.stack([image_grad, text_grad]), units, lengths)
    block_own = as_lies(block_own)
    block_own, preact = lax.optimization_barrier((block_own, preact))
    far = swap(block_own, "xh")
    _, gelu_back = jax.vjp(gelu_tanh, preact)
    slope = gelu_back(jnp.ones_like(preact))[0]
    far, slope = lax.optimization_barrier((far, slope))
    block_low = as_lies(in_order(block_own, far, "xh", 1))
    block_low = as_lies(swap_join(block_low, "c", 1))
    hidden_grad = jnp.einsum("kte,kfe->ktf", block_low, fc2, preferred_element_type=F32)
    preact_grad = lax.optimization_barrier((hidden_grad * slope).astype(BF))
    normed_grad = jnp.einsum("ktf,kdf->ktd", preact_grad, fc1, preferred_element_type=F32)
    scaled = normed_grad * gains
    norm_term = (
        scaled
        - jnp.mean(scaled, axis=-1, keepdims=True)
        - standard * jnp.mean(scaled * standard, axis=-1, keepdims=True)
    ) * inverse
    norm_parts = as_lies(jnp.swapaxes(norm_term, 1, 2)).reshape(2, 2, 2, width, rows)
    norm_parts = as_lies(swap_sum(norm_parts, "c", 2))
    norm_share = as_lies(swap_sum(norm_parts, "xh", 1))
    block_share = as_lies(lax.dynamic_slice_in_dim(block_low, member * width, width, 2))
    block_share = as_lies(jnp.swapaxes(block_share, 1, 2)).astype(F32)
    return jnp.swapaxes(as_lies((block_share + norm_share).astype(BF)), 1, 2)


def solution(mesh):
    fine = Mesh(mesh.devices.reshape(4, 8, 2, 2, 2), ("y", "z", "xl", "xh", "c"))
    in_specs = (
        P(None, DP, TENSOR),
        P(),
        P(),
        P(None, None, TENSOR),
        P(None, TENSOR),
        P(None, TENSOR, None),
        P(),
        P(),
        P(),
        P(),
    )
    return jax.shard_map(
        on_device, mesh=fine, in_specs=in_specs, out_specs=P(None, DP, TENSOR), check_vma=False
    )
```
